32 devices in a mesh: seq: 8 (over z, y), head: 4 (over x, core).
Axes of the slice: x: 2, y: 2, z: 4, core: 2. Of those that a mesh axis runs over, the one named last changes fastest.
Arguments:
- query_rows: bfloat16 [6144, 2048], P('seq', 'head'), may hold values from -6 to 6
- key_rows: bfloat16 [6144, 2048], P('seq', 'head'), may hold values from -6 to 6
- value_rows: bfloat16 [6144, 2048], P('seq', 'head'), may hold values from -6 to 6
- output_rows: bfloat16 [6144, 2048], P('seq', 'head'), may hold values from -6 to 6
- output_grad: bfloat16 [6144, 2048], P('seq', 'head'), may hold values from -6 to 6
- projection: bfloat16 [3, 2048, 3072], P(None, 'head'), may hold values from -0.078125 to 0.078125
- neighbours: int32 [16, 4], replicated, may hold values from 0 to 15, as said below
- counts: int32 [16], replicated, may hold values from 3 to 4, as said below
Outputs:
- input_grad: bfloat16 [6144, 3072], P('seq', 'head')
The draws below stay inside these ranges and needn't reach their ends.
Inputs may be any that keep to these rules, and one draw needn't show every extreme that they name: `neighbours`: row t lists 4 different tiles: first t itself, then t - 1, then t + 1 (modulo 16); the others lie among tiles (t // 2 - 1) * 2 to (t // 2 + 2) * 2 - 1, taken modulo 16. `counts`: every tile uses at least its first three listed tiles; some tile uses all 4.
All inputs are finite; a program needn't handle non-finite values.
Results may differ from the reference program's by a relative error of at most 0.015.
Values may be sent and summed in bfloat16 or wider, within the bound.
A program may use at most 128 MiB of HBM per device.

```python
import jax
import jax.numpy as jnp
from jax import lax

DM = 3072
HEADS = 16
HD = 128
TILE = 384
NB = 4
TILES_DEV = 2
NTILES = 16
TOKENS = 6144
N_HEAD = 4


def draw_neighbours(key, part):
    tile_ids = jnp.arange(NTILES)
    home = tile_ids // TILES_DEV
    places = jnp.arange(3 * TILES_DEV)
    window = (home[:, None] * TILES_DEV - TILES_DEV + places[None, :]) % NTILES
    own_slot = TILES_DEV + tile_ids % TILES_DEV
    ranks = jax.random.randint(key, (NTILES, 3 * TILES_DEV), 0, 1 << 20) * (3 * TILES_DEV) + places[None, :]
    ranks = jnp.where(places[None, :] == own_slot[:, None], -3, ranks)
    ranks = jnp.where(places[None, :] == own_slot[:, None] - 1, -2, ranks)
    ranks = jnp.where(places[None, :] == own_slot[:, None] + 1, -1, ranks)
    order = jnp.argsort(ranks, axis=1)
    return jnp.take_along_axis(window, order[:, :NB], axis=1).astype(jnp.int32)


def draw_counts(key, part):
    drawn = jax.random.randint(key, (NTILES,), 3, NB + 1)
    return drawn.at[0].set(NB).astype(jnp.int32)


def draw_query_rows(key, part):
    shape = (TOKENS, HEADS * HD)
    noise = 0.4 * jax.random.normal(jax.random.fold_in(key, 1), shape, jnp.float32)
    return noise.astype(jnp.bfloat16)


def draw_key_rows(key, part):
    shape = (TOKENS, HEADS * HD)
    noise = 0.4 * jax.random.normal(jax.random.fold_in(key, 2), shape, jnp.float32)
    return noise.astype(jnp.bfloat16)


def shard_levels(own_key, dims, shards, least, high):
    level = 1.0
    for dim, parts in shards:
        draws = jax.random.uniform(jax.random.fold_in(jax.random.fold_in(own_key, 6), dim), (parts,), jnp.float32, least / len(shards), high / len(shards))
        level = level * jnp.repeat(jnp.exp(draws), dims[dim] // parts).reshape((-1,) + (1,) * (len(dims) - 1 - dim))
    return level


def centred(rng, shape, width, limit, cuts=(), dtype=jnp.bfloat16):
    values = width * jax.random.normal(rng, shape, jnp.float32)
    if cuts:
        values = values * shard_levels(rng, shape, cuts, -0.22, 0.18)
    return jnp.clip(values, -limit, limit).astype(dtype)


def setup_inputs(seed: int = 0) -> dict:
    streams_of = jax.random.split(jax.random.key(seed), 9)
    return {
        "query_rows": draw_query_rows(jax.random.fold_in(streams_of[8], 71), 0),
        "key_rows": draw_key_rows(jax.random.fold_in(streams_of[8], 71), 0),
        "value_rows": centred(streams_of[2], (TOKENS, HEADS * HD), 1.0, 6.0, ((0, 8), (1, 4))),
        "output_rows": centred(streams_of[3], (TOKENS, HEADS * HD), 1.0, 6.0, ((0, 8), (1, 4))),
        "output_grad": centred(streams_of[4], (TOKENS, HEADS * HD), 1.0, 6.0, ((0, 8), (1, 4))),
        "projection": centred(streams_of[5], (3, HEADS * HD, DM), (3 * HEADS * HD) ** -0.5, 0.078125, ((1, 4),)),
        "neighbours": draw_neighbours(jax.random.fold_in(streams_of[8], 71), 0),
        "counts": draw_counts(jax.random.fold_in(streams_of[8], 71), 0),
    }


def reference(query_rows, key_rows, value_rows, output_rows, output_grad, projection, neighbours, counts):
    score_scale = HD ** -0.5
    group_size = HEADS // N_HEAD

    def per_head(carry, head_at):
        total, group_acc = carry
        offset = (head_at * HD).astype(jnp.int32)

        def select(array):
            return lax.dynamic_slice_in_dim(array, offset, HD, 1).reshape(NTILES, TILE, HD)

        queries = select(query_rows)
        keys_all = select(key_rows)
        values_all = select(value_rows)
        outputs = select(output_rows)
        grads_out = select(output_grad)
        deltas = jnp.sum(grads_out.astype(jnp.float32) * outputs.astype(jnp.float32), axis=-1)

        def per_tile(partials, tile_at):
            key_acc, value_acc = partials
            listed = neighbours[tile_at]
            is_live = jnp.arange(NB) < counts[tile_at]
            live_mask = is_live[None, :, None]
            near_keys = keys_all[listed].astype(jnp.float32)
            near_values = values_all[listed].astype(jnp.float32)
            query_tile = queries[tile_at].astype(jnp.float32)
            grad_tile = grads_out[tile_at].astype(jnp.float32)
            scores = jnp.einsum("id,jcd->ijc", query_tile, near_keys) * score_scale
            scores = jnp.where(live_mask, scores, -jnp.inf)
            row_peak = jnp.max(scores, axis=(1, 2))
            raised = jnp.where(live_mask, jnp.exp(scores - row_peak[:, None, None]), 0.0)
            row_total = jnp.sum(raised, axis=(1, 2))
            softmax_weights = (raised / row_total[:, None, None]).astype(jnp.bfloat16)
            prob_grad = jnp.einsum("id,jcd->ijc", grad_tile, near_values)
            score_grad = (softmax_weights.astype(jnp.float32) * (prob_grad - deltas[tile_at][:, None, None]) * score_scale).astype(jnp.bfloat16)
            query_grad = jnp.einsum("ijc,jcd->id", score_grad.astype(jnp.float32), near_keys).astype(jnp.bfloat16)
            key_part = jnp.einsum("ijc,id->jcd", score_grad.astype(jnp.float32), query_tile)
            value_part = jnp.einsum("ijc,id->jcd", softmax_weights.astype(jnp.float32), grad_tile)
            return (key_acc.at[listed].add(key_part), value_acc.at[listed].add(value_part)), query_grad

        zero_tiles = jnp.zeros((NTILES, TILE, HD), jnp.float32)
        (key_acc, value_acc), query_grad = lax.scan(per_tile, (zero_tiles, zero_tiles), jnp.arange(NTILES))
        stacked = jnp.stack([query_grad.reshape(TOKENS, HD), key_acc.astype(jnp.bfloat16).reshape(TOKENS, HD), value_acc.astype(jnp.bfloat16).reshape(TOKENS, HD)])
        weight = lax.dynamic_slice_in_dim(projection, offset, HD, 1)
        group_acc = group_acc + jnp.einsum("cik,ckm->im", stacked.astype(jnp.float32), weight.astype(jnp.float32))
        is_end = (head_at + 1) % group_size == 0
        rounded = lax.optimization_barrier(group_acc.astype(jnp.bfloat16)).astype(jnp.float32)
        total = total + jnp.where(is_end, rounded, jnp.float32(0.0))
        group_acc = jnp.where(is_end, jnp.float32(0.0), group_acc)
        return (total, group_acc), None

    zero_rows = jnp.zeros((TOKENS, DM), jnp.float32)
    (total, _), _ = lax.scan(per_head, (zero_rows, zero_rows), jnp.arange(HEADS))
    return total.astype(jnp.bfloat16)
```

```python
import functools
import math

import jax
import jax.numpy as jnp
from jax import lax
from jax.experimental import pallas as pl
from jax.experimental.pallas import tpu as pltpu
from jax.sharding import PartitionSpec as P

HD = 128
TILE = 384
NB = 4
HALO = 2
F32 = jnp.float32
BF16 = jnp.bfloat16


def dot(a, b, dims):
    return lax.dot_general(a, b, ((dims[:1], dims[1:]), ((), ())), preferred_element_type=F32)


def attention_kernel(
    tiles, own_blocks, slots_ref, counts_ref, delta_ref, *refs
):
    qg_refs = refs[:own_blocks]
    kv_refs = refs[own_blocks : 2 * own_blocks + 2]
    query_grad_ref, prev_ref, own_ref, next_ref = refs[2 * own_blocks + 2 : 2 * own_blocks + 6]
    qg, kv, key_acc, value_acc, work = refs[2 * own_blocks + 6 :]
    rows_block = HALO * TILE
    for at, ref in enumerate(qg_refs):
        qg[at * rows_block : (at + 1) * rows_block, :] = ref[...]
    for at, ref in enumerate(kv_refs):
        kv[at * rows_block : (at + 1) * rows_block, :] = ref[...]
    key_acc[...] = jnp.zeros_like(key_acc)
    value_acc[...] = jnp.zeros_like(value_acc)
    scale = HD ** (-0.5)
    exponent = scale * math.log2(math.e)

    def tile_step(tile, slot_places):
        base = pl.multiple_of(tile * TILE, TILE)
        query = qg[pl.ds(base, TILE), :HD]
        grad = qg[pl.ds(base, TILE), HD:]
        delta = delta_ref[tile]
        starts = [pl.multiple_of(place * TILE, TILE) for place in slot_places]
        peak = None
        for j, start in enumerate(starts):
            scores = dot(kv[pl.ds(start, TILE), :HD], query, (1, 1))
            work[j] = scores
            top = jnp.max(scores, axis=0, keepdims=True)
            peak = top if peak is None else jnp.maximum(peak, top)
        total = jnp.zeros_like(peak)
        for j in range(len(starts)):
            raised = jnp.exp2((work[j] - peak) * exponent)
            work[j] = raised
            total = total + jnp.sum(raised, axis=0, keepdims=True)
        inverse = 1.0 / total
        query_grad = jnp.zeros((HD, TILE), F32)
        for j, start in enumerate(starts):
            keys = kv[pl.ds(start, TILE), :HD]
            weights = (work[j] * inverse).astype(BF16)
            prob_grad = dot(kv[pl.ds(start, TILE), HD:], grad, (1, 1))
            score_grad = (weights.astype(F32) * ((prob_grad - delta) * scale)).astype(BF16)
            value_acc[pl.ds(start, TILE), :] += dot(weights, grad, (1, 0))
            key_acc[pl.ds(start, TILE), :] += dot(score_grad, query, (1, 0))
            query_grad = query_grad + dot(keys, score_grad, (0, 0))
        query_grad_ref[pl.ds(base, TILE), :] = query_grad.T.astype(BF16)

    @pl.loop(0, tiles)
    def _(tile):
        near = [tile + HALO, tile + HALO - 1, tile + HALO + 1]

        @pl.when(counts_ref[tile] >= NB)
        def _():
            tile_step(tile, near + [slots_ref[tile * NB + NB - 1]])

        @pl.when(counts_ref[tile] < NB)
        def _():
            tile_step(tile, near)

    end = own_blocks + 1
    for half, acc in enumerate((key_acc, value_acc)):
        cols = slice(half * HD, (half + 1) * HD)
        prev_ref[:, cols] = acc[:rows_block, :].astype(BF16)
        own_ref[:, cols] = acc[rows_block : end * rows_block, :]
        next_ref[:, cols] = acc[end * rows_block :, :].astype(BF16)


def attention(slots, counts, delta, qg_blocks, kv_blocks):
    own_blocks = len(qg_blocks)
    tiles = own_blocks * HALO
    rows = tiles * TILE
    rows_block = HALO * TILE
    window = rows + 2 * rows_block
    vmem = pl.BlockSpec(memory_space=pltpu.VMEM)
    smem = pl.BlockSpec(memory_space=pltpu.SMEM)
    pair = jax.ShapeDtypeStruct((rows_block, 2 * HD), BF16)
    return pl.pallas_call(
        functools.partial(attention_kernel, tiles, own_blocks),
        out_shape=[
            jax.ShapeDtypeStruct((rows, HD), BF16),
            pair,
            jax.ShapeDtypeStruct((rows, 2 * HD), F32),
            pair,
        ],
        in_specs=[smem, smem] + [vmem] * (1 + len(qg_blocks) + len(kv_blocks)),
        out_specs=[vmem] * 4,
        scratch_shapes=[
            pltpu.VMEM((rows, 2 * HD), BF16),
            pltpu.VMEM((window, 2 * HD), BF16),
            pltpu.VMEM((window, HD), F32),
            pltpu.VMEM((window, HD), F32),
            pltpu.VMEM((NB, TILE, TILE), F32),
        ],
        compiler_params=pltpu.CompilerParams(vmem_limit_bytes=40 * 2**20),
        cost_estimate=pl.CostEstimate(
            flops=2 * 5 * rows * NB * TILE * HD * 2,
            bytes_accessed=rows * HD * 30,
            transcendentals=rows * NB * TILE,
        ),
    )(slots.reshape(-1), counts, delta.reshape(tiles, 1, TILE), *qg_blocks, *kv_blocks)


def shifted(block, axis, distance):
    count = lax.axis_size(axis)
    return lax.ppermute(block, axis, [(i, (i + distance) % count) for i in range(count)])


def swapped(block, axis, bit):
    count = lax.axis_size(axis)
    return lax.ppermute(block, axis, [(i, i ^ bit) for i in range(count)])


def head_cols(array, head):
    return lax.dynamic_slice_in_dim(array, head * HD, HD, 1)


def tables(neighbours, counts, first, tiles, tiles_all):
    ids = first + jnp.arange(tiles)
    slots = (neighbours[ids] - (first - HALO)) % tiles_all
    return slots.astype(jnp.int32), counts[ids].astype(jnp.int32)


def summed_over_heads(grads, projection):
    stack = jnp.stack(grads)
    count = lax.axis_size("head")
    if count != 4:
        term = jnp.einsum("cik,ckm->im", stack, projection, preferred_element_type=F32)
        return lax.psum_scatter(term.astype(BF16), "head", scatter_dimension=1, tiled=True)
    place = lax.axis_index("head")
    chip, core = place // 2, place % 2
    width = projection.shape[2] // count

    def chip_sum(target):
        weights = lax.dynamic_slice_in_dim(projection, target * 2 * width, 2 * width, 2)
        term = jnp.einsum("cik,ckm->im", stack, weights, preferred_element_type=F32).astype(BF16)
        sent = lax.dynamic_slice_in_dim(term, (1 - core) * width, width, 1)
        kept = lax.dynamic_slice_in_dim(term, core * width, width, 1)
        return kept.astype(F32) + swapped(sent, "head", 1).astype(F32)

    far = swapped(chip_sum(1 - chip).astype(BF16), "head", 2)
    return (chip_sum(chip) + far.astype(F32)).astype(BF16)


def local(
    query_rows, key_rows, value_rows, output_rows, output_grad, projection, neighbours, counts
):
    seq_count = lax.axis_size("seq")
    place = lax.axis_index("seq")
    rows_dev = query_rows.shape[0]
    tiles_dev = rows_dev // TILE
    tiles_all = tiles_dev * seq_count
    heads_dev = query_rows.shape[1] // HD
    deltas = jnp.sum(
        (output_grad.astype(F32) * output_rows.astype(F32)).reshape(rows_dev, heads_dev, HD), axis=-1
    ).T
    grads = ([], [], [])
    if heads_dev % 2 or seq_count % 2:
        slots, live = tables(neighbours, counts, place * tiles_dev, tiles_dev, tiles_all)
        for head in range(heads_dev):
            qg = jnp.concatenate([head_cols(query_rows, head), head_cols(output_grad, head)], 1)
            kv = jnp.concatenate([head_cols(key_rows, head), head_cols(value_rows, head)], 1)
            window = [shifted(kv, "seq", 1), kv, shifted(kv, "seq", -1)]
            query_grad, to_prev, own, to_next = attention(slots, live, deltas[head], [qg], window)
            own = (
                own + shifted(to_prev, "seq", -1).astype(F32) + shifted(to_next, "seq", 1).astype(F32)
            ).astype(BF16)
            for into, block in zip(grads, (query_grad, own[:, :HD], own[:, HD:])):
                into.append(block)
        return summed_over_heads([jnp.concatenate(blocks, 1) for blocks in grads], projection)

    odd = place % 2
    half = heads_dev // 2
    first = (place - odd) * tiles_dev
    slots, live = tables(neighbours, counts, first, 2 * tiles_dev, tiles_all)

    def in_order(mine, other):
        return jnp.where(odd == 0, mine, other), jnp.where(odd == 0, other, mine)

    delta_mine = lax.dynamic_slice_in_dim(deltas, odd * half, half, 0)
    delta_sent = lax.dynamic_slice_in_dim(deltas, (1 - odd) * half, half, 0)
    delta_pair = jnp.concatenate(in_order(delta_mine, swapped(delta_sent, "seq", 1)), 1)

    def exchanged(left, right, step):
        def both(head):
            return jnp.concatenate([head_cols(left, head), head_cols(right, head)], 1)

        return in_order(
            both(odd * half + step), swapped(both((1 - odd) * half + step), "seq", 1)
        )

    mine, other = [], []
    kv_pairs = [exchanged(key_rows, value_rows, step) for step in range(half)]
    qg_pairs = [exchanged(query_rows, output_grad, step) for step in range(half)]
    for step in range(half):
        low, high = kv_pairs[step]
        window = [shifted(high, "seq", 2), low, high, shifted(low, "seq", -2)]
        query_grad, to_prev, own, to_next = attention(
            slots, live, delta_pair[step], list(qg_pairs[step]), window
        )
        from_next = shifted(to_prev, "seq", -2)
        from_prev = shifted(to_next, "seq", 2)
        low = own[:rows_dev] + from_prev.astype(F32)
        high = own[rows_dev:] + from_next.astype(F32)
        low = jnp.concatenate([query_grad[:rows_dev], low.astype(BF16)], 1)
        high = jnp.concatenate([query_grad[rows_dev:], high.astype(BF16)], 1)
        mine.append(jnp.where(odd == 0, low, high))
        other.append(swapped(jnp.where(odd == 0, high, low), "seq", 1))
    parts = []
    for which in range(3):
        cols = slice(which * HD, (which + 1) * HD)
        first_half, second_half = in_order(
            jnp.concatenate([block[:, cols] for block in mine], 1),
            jnp.concatenate([block[:, cols] for block in other], 1),
        )
        parts.append(jnp.concatenate([first_half, second_half], 1))
    return summed_over_heads(parts, projection)


def solution(mesh):
    in_specs = (
        P("seq", "head"),
        P("seq", "head"),
        P("seq", "head"),
        P("seq", "head"),
        P("seq", "head"),
        P(None, "head", None),
        P(),
        P(),
    )
    out_specs = P("seq", "head")
    return jax.shard_map(local, mesh=mesh, in_specs=in_specs, out_specs=out_specs, check_vma=False)
```

```python
import functools
import math

import jax
import jax.numpy as jnp
from jax import lax
from jax.experimental import pallas as pl
from jax.experimental.pallas import tpu as pltpu
from jax.sharding import PartitionSpec as P

HD = 128
TILE = 384
NB = 4
HALO = 2
F32 = jnp.float32
BF16 = jnp.bfloat16


def dot(a, b, dims):
    return lax.dot_general(a, b, ((dims[:1], dims[1:]), ((), ())), preferred_element_type=F32)


def attention_kernel(
    tiles, own_blocks, slots_ref, counts_ref, delta_ref, *refs
):
    qg_refs = refs[:own_blocks]
    kv_refs = refs[own_blocks : 2 * own_blocks + 2]
    query_grad_ref, prev_ref, own_ref, next_ref = refs[2 * own_blocks + 2 : 2 * own_blocks + 6]
    qg, kv, key_acc, value_acc, work = refs[2 * own_blocks + 6 :]
    rows_block = HALO * TILE
    for at, ref in enumerate(qg_refs):
        qg[at * rows_block : (at + 1) * rows_block, :] = ref[...]
    for at, ref in enumerate(kv_refs):
        kv[at * rows_block : (at + 1) * rows_block, :] = ref[...]
    key_acc[...] = jnp.zeros_like(key_acc)
    value_acc[...] = jnp.zeros_like(value_acc)
    scale = HD ** (-0.5)
    exponent = scale * math.log2(math.e)

    def tile_step(tile, slot_places):
        base = pl.multiple_of(tile * TILE, TILE)
        query = qg[pl.ds(base, TILE), :HD]
        grad = qg[pl.ds(base, TILE), HD:]
        delta = delta_ref[tile]
        starts = [pl.multiple_of(place * TILE, TILE) for place in slot_places]
        peak = None
        for j, start in enumerate(starts):
            scores = dot(kv[pl.ds(start, TILE), :HD], query, (1, 1))
            work[j] = scores
            top = jnp.max(scores, axis=0, keepdims=True)
            peak = top if peak is None else jnp.maximum(peak, top)
        total = jnp.zeros_like(peak)
        for j in range(len(starts)):
            raised = jnp.exp2((work[j] - peak) * exponent)
            work[j] = raised
            total = total + jnp.sum(raised, axis=0, keepdims=True)
        inverse = 1.0 / total
        query_grad = jnp.zeros((HD, TILE), F32)
        for j, start in enumerate(starts):
            keys = kv[pl.ds(start, TILE), :HD]
            weights = (work[j] * inverse).astype(BF16)
            prob_grad = dot(kv[pl.ds(start, TILE), HD:], grad, (1, 1))
            score_grad = (weights.astype(F32) * ((prob_grad - delta) * scale)).astype(BF16)
            value_acc[pl.ds(start, TILE), :] += dot(weights, grad, (1, 0))
            key_acc[pl.ds(start, TILE), :] += dot(score_grad, query, (1, 0))
            query_grad = query_grad + dot(keys, score_grad, (0, 0))
        query_grad_ref[pl.ds(base, TILE), :] = query_grad.T.astype(BF16)

    @pl.loop(0, tiles)
    def _(tile):
        near = [tile + HALO, tile + HALO - 1, tile + HALO + 1]

        @pl.when(counts_ref[tile] >= NB)
        def _():
            tile_step(tile, near + [slots_ref[tile * NB + NB - 1]])

        @pl.when(counts_ref[tile] < NB)
        def _():
            tile_step(tile, near)

    end = own_blocks + 1
    for half, acc in enumerate((key_acc, value_acc)):
        cols = slice(half * HD, (half + 1) * HD)
        own_ref[:, cols] = acc[rows_block : end * rows_block, :]
        for at in range(HALO):
            before = (HALO - 1 - at) * TILE
            after = end * rows_block + at * TILE
            prev_ref[at, :, cols] = acc[before : before + TILE, :].astype(BF16)
            next_ref[at, :, cols] = acc[after : after + TILE, :].astype(BF16)


def attention(slots, counts, delta, qg_blocks, kv_blocks):
    own_blocks = len(qg_blocks)
    tiles = own_blocks * HALO
    rows = tiles * TILE
    rows_block = HALO * TILE
    window = rows + 2 * rows_block
    vmem = pl.BlockSpec(memory_space=pltpu.VMEM)
    smem = pl.BlockSpec(memory_space=pltpu.SMEM)
    pair = jax.ShapeDtypeStruct((HALO, TILE, 2 * HD), BF16)
    return pl.pallas_call(
        functools.partial(attention_kernel, tiles, own_blocks),
        out_shape=[
            jax.ShapeDtypeStruct((rows, HD), BF16),
            pair,
            jax.ShapeDtypeStruct((rows, 2 * HD), F32),
            pair,
        ],
        in_specs=[smem, smem] + [vmem] * (1 + len(qg_blocks) + len(kv_blocks)),
        out_specs=[vmem] * 4,
        scratch_shapes=[
            pltpu.VMEM((rows, 2 * HD), BF16),
            pltpu.VMEM((window, 2 * HD), BF16),
            pltpu.VMEM((window, HD), F32),
            pltpu.VMEM((window, HD), F32),
            pltpu.VMEM((NB, TILE, TILE), F32),
        ],
        compiler_params=pltpu.CompilerParams(vmem_limit_bytes=40 * 2**20),
        cost_estimate=pl.CostEstimate(
            flops=2 * 5 * rows * NB * TILE * HD * 2,
            bytes_accessed=rows * HD * 30,
            transcendentals=rows * NB * TILE,
        ),
    )(slots.reshape(-1), counts, delta.reshape(tiles, 1, TILE), *qg_blocks, *kv_blocks)


def shifted(block, axis, distance):
    count = lax.axis_size(axis)
    return lax.ppermute(block, axis, [(i, (i + distance) % count) for i in range(count)])


def swapped(block, axis, bit):
    count = lax.axis_size(axis)
    return lax.ppermute(block, axis, [(i, i ^ bit) for i in range(count)])


def head_cols(array, head):
    return lax.dynamic_slice_in_dim(array, head * HD, HD, 1)


def tables(neighbours, counts, first, tiles, tiles_all):
    ids = first + jnp.arange(tiles)
    slots = (neighbours[ids] - (first - HALO)) % tiles_all
    return slots.astype(jnp.int32), counts[ids].astype(jnp.int32)


def owner_terms(stack, projection):
    count = lax.axis_size("head")
    place = lax.axis_index("head")
    chip, core = place // 2, place % 2
    width = projection.shape[2] // count

    def chip_sum(target):
        weights = lax.dynamic_slice_in_dim(projection, target * 2 * width, 2 * width, 2)
        term = jnp.einsum("cik,ckm->im", stack, weights, preferred_element_type=F32).astype(BF16)
        sent = lax.dynamic_slice_in_dim(term, (1 - core) * width, width, 1)
        kept = lax.dynamic_slice_in_dim(term, core * width, width, 1)
        return kept.astype(F32) + swapped(sent, "head", 1).astype(F32)

    far = swapped(chip_sum(1 - chip).astype(BF16), "head", 2)
    return chip_sum(chip), far


def scattered_over_heads(stack, projection):
    term = jnp.einsum("cik,ckm->im", stack, projection, preferred_element_type=F32)
    return lax.psum_scatter(term.astype(BF16), "head", scatter_dimension=1, tiled=True)


def after(arrays, awaited):
    return lax.optimization_barrier((tuple(arrays), tuple(awaited)))[0]


def tile_of(array, at):
    return lax.slice_in_dim(array, at * TILE, (at + 1) * TILE, axis=0)


def local(
    query_rows, key_rows, value_rows, output_rows, output_grad, projection, neighbours, counts
):
    seq_count = lax.axis_size("seq")
    place = lax.axis_index("seq")
    rows_dev = query_rows.shape[0]
    tiles_dev = rows_dev // TILE
    tiles_all = tiles_dev * seq_count
    heads_dev = query_rows.shape[1] // HD
    deltas = jnp.sum(
        (output_grad.astype(F32) * output_rows.astype(F32)).reshape(rows_dev, heads_dev, HD), axis=-1
    ).T
    if heads_dev % 2 or seq_count % 2 or tiles_dev != HALO:
        grads = ([], [], [])
        slots, live = tables(neighbours, counts, place * tiles_dev, tiles_dev, tiles_all)
        for head in range(heads_dev):
            qg = jnp.concatenate([head_cols(query_rows, head), head_cols(output_grad, head)], 1)
            kv = jnp.concatenate([head_cols(key_rows, head), head_cols(value_rows, head)], 1)
            window = [shifted(kv, "seq", 1), kv, shifted(kv, "seq", -1)]
            query_grad, to_prev, own, to_next = attention(slots, live, deltas[head], [qg], window)
            from_next = shifted(to_prev, "seq", -1)[::-1].reshape(rows_dev, 2 * HD)
            from_prev = shifted(to_next, "seq", 1).reshape(rows_dev, 2 * HD)
            own = (own + from_next.astype(F32) + from_prev.astype(F32)).astype(BF16)
            for into, block in zip(grads, (query_grad, own[:, :HD], own[:, HD:])):
                into.append(block)
        stack = jnp.stack([jnp.concatenate(blocks, 1) for blocks in grads])
        return scattered_over_heads(stack, projection)

    odd = place % 2
    even = odd == 0
    half = heads_dev // 2
    first = (place - odd) * tiles_dev
    slots, live = tables(neighbours, counts, first, 2 * tiles_dev, tiles_all)

    def in_order(mine, other):
        return jnp.where(even, mine, other), jnp.where(even, other, mine)

    def both(left, right, head):
        return jnp.concatenate([head_cols(left, head), head_cols(right, head)], 1)

    kept, sent = odd * half, (1 - odd) * half
    kv_kept = [both(key_rows, value_rows, kept + step) for step in range(half)]
    kv_sent = [both(key_rows, value_rows, sent + step) for step in range(half)]
    qg_kept = [both(query_rows, output_grad, kept + step) for step in range(half)]
    qg_sent = [both(query_rows, output_grad, sent + step) for step in range(half)]

    kv_got = [swapped(kv_sent[0], "seq", 1)]
    delta_sent = lax.dynamic_slice_in_dim(deltas, sent, half, 0)
    qg_got = []
    for step in range(half):
        awaited = kv_got[step]
        wave = [qg_sent[step]] + kv_sent[step + 1 : step + 2]
        if step == 0:
            wave.append(delta_sent)
        wave = [swapped(block, "seq", 1) for block in after(wave, [awaited])]
        qg_got.append(wave[0])
        if step + 1 < half:
            kv_got.append(wave[1])
        if step == 0:
            delta_got = wave[-1]
    delta_kept = lax.dynamic_slice_in_dim(deltas, kept, half, 0)
    delta_pair = jnp.concatenate(in_order(delta_kept, delta_got), 1)

    kv_pairs = [in_order(kv_kept[step], kv_got[step]) for step in range(half)]
    halos = []
    for step in range(half):
        ends = kv_pairs[step] if step == 0 else after(kv_pairs[step], halos[-1])
        halos.append((shifted(ends[1], "seq", 2), shifted(ends[0], "seq", -2)))

    def of_owner(tiles_low_high):
        low, high = tiles_low_high
        return jnp.where(even, low, high), jnp.where(even, high, low)

    places = ((0, 3), (1, 2))
    query_grads, kv_mine, kv_other = [], [], []
    arrived = None
    for step in range(half):
        low, high = kv_pairs[step]
        window = [halos[step][0], low, high, halos[step][1]]
        qg_blocks = list(in_order(qg_kept[step], qg_got[step]))
        query_grad, to_prev, own, to_next = attention(
            slots, live, delta_pair[step], qg_blocks, window
        )
        query_grads.append(query_grad)
        if step + 1 < half:
            to_prev, to_next = after((to_prev, to_next), halos[step + 1])
            back = shifted(to_prev, "seq", -2), shifted(to_next, "seq", 2)
            from_next, from_prev = [[block[at] for at in range(HALO)] for block in back]
        else:
            ends = [(to_prev[at], to_next[at]) for at in range(HALO)]
            from_next, from_prev = [], []
            for at in range(HALO):
                block = after(ends[at], arrived) if arrived else ends[at]
                arrived = shifted(block[0], "seq", -2), shifted(block[1], "seq", 2)
                from_next.append(arrived[0])
                from_prev.append(arrived[1])
        if step + 1 < half:
            arrived = back
        sums = []
        for at, (at_low, at_high) in enumerate(places):
            low = tile_of(own, at_low) + from_prev[at].astype(F32)
            high = tile_of(own, at_high) + from_next[at].astype(F32)
            sums.append(of_owner((low.astype(BF16), high.astype(BF16))))
        kv_mine.append([mine for mine, _ in sums])
        if step + 1 < half:
            got = swapped(jnp.concatenate([other for _, other in sums], 0), "seq", 1)
            kv_other.append([tile_of(got, at) for at in range(HALO)])
        else:
            kv_other.append([swapped(other, "seq", 1) for _, other in sums])
    query_all = jnp.concatenate(query_grads, 1)
    query_sums = [of_owner((tile_of(query_all, low), tile_of(query_all, high))) for low, high in places]
    query_got = swapped(jnp.concatenate([other for _, other in query_sums], 0), "seq", 1)

    results = []
    for at in range(HALO):
        parts = [in_order(query_sums[at][0], tile_of(query_got, at))]
        for cols in (slice(0, HD), slice(HD, 2 * HD)):
            parts.append(
                in_order(
                    jnp.concatenate([blocks[at][:, cols] for blocks in kv_mine], 1),
                    jnp.concatenate([blocks[at][:, cols] for blocks in kv_other], 1),
                )
            )
        stack = jnp.stack([jnp.concatenate(part, 1) for part in parts])
        if lax.axis_size("head") == 4:
            near, far = owner_terms(stack, projection)
            results.append((near + far.astype(F32)).astype(BF16))
        else:
            results.append(scattered_over_heads(stack, projection))
    return jnp.concatenate(in_order(results[0], results[1]), 0)


def solution(mesh):
    in_specs = (
        P("seq", "head"),
        P("seq", "head"),
        P("seq", "head"),
        P("seq", "head"),
        P("seq", "head"),
        P(None, "head", None),
        P(),
        P(),
    )
    out_specs = P("seq", "head")
    return jax.shard_map(local, mesh=mesh, in_specs=in_specs, out_specs=out_specs, check_vma=False)
```

```python
import functools
import math

import jax
import jax.numpy as jnp
from jax import lax
from jax.experimental import pallas as pl
from jax.experimental.pallas import tpu as pltpu
from jax.sharding import PartitionSpec as P

HD = 128
TILE = 384
NB = 4
HALO = 2
F32 = jnp.float32
BF16 = jnp.bfloat16


def dot(a, b, dims):
    return lax.dot_general(a, b, ((dims[:1], dims[1:]), ((), ())), preferred_element_type=F32)


def attention_kernel(own_blocks, slots_ref, counts_ref, odd_ref, delta_ref, *refs):
    n = own_blocks
    tiles = n * HALO
    qg_refs, kv_refs, refs = refs[:n], refs[n : 2 * n + 2], refs[2 * n + 2 :]
    query_grad_refs, kv_grad_refs, refs = refs[:n], refs[n : 2 * n + 2], refs[2 * n + 2 :]
    qg, kv, query_acc, key_acc, value_acc, work = refs
    rows_block = HALO * TILE
    if n == 2:
        odd = odd_ref[0]
        places = [1 + odd, 2 - odd, 3 * (1 - odd), 3 * odd]
        flips = [odd, 1 - odd, odd, 1 - odd]
    else:
        places, flips = [1, 0, 2], [0, 0, 0]

    def tile_rows(place, flip, at):
        in_block = flip if at == 0 else 1 - flip
        return pl.ds(pl.multiple_of((place * HALO + in_block) * TILE, TILE), TILE)

    for place, ref in zip(places, qg_refs):
        qg[pl.ds(pl.multiple_of((place - 1) * rows_block, TILE), rows_block), :] = ref[...]
    for place, ref in zip(places, kv_refs):
        kv[pl.ds(pl.multiple_of(place * rows_block, TILE), rows_block), :] = ref[...]
    key_acc[...] = jnp.zeros_like(key_acc)
    value_acc[...] = jnp.zeros_like(value_acc)
    scale = HD ** (-0.5)
    exponent = scale * math.log2(math.e)

    def tile_step(tile, slot_places):
        base = pl.multiple_of(tile * TILE, TILE)
        query = qg[pl.ds(base, TILE), :HD]
        grad = qg[pl.ds(base, TILE), HD:]
        delta = delta_ref[tile]
        starts = [pl.multiple_of(place * TILE, TILE) for place in slot_places]
        peak = None
        for j, start in enumerate(starts):
            scores = dot(kv[pl.ds(start, TILE), :HD], query, (1, 1))
            work[j] = scores
            top = jnp.max(scores, axis=0, keepdims=True)
            peak = top if peak is None else jnp.maximum(peak, top)
        total = jnp.zeros_like(peak)
        for j in range(len(starts)):
            raised = jnp.exp2((work[j] - peak) * exponent)
            work[j] = raised
            total = total + jnp.sum(raised, axis=0, keepdims=True)
        inverse = 1.0 / total
        query_grad = jnp.zeros((HD, TILE), F32)
        for j, start in enumerate(starts):
            keys = kv[pl.ds(start, TILE), :HD]
            weights = (work[j] * inverse).astype(BF16)
            prob_grad = dot(kv[pl.ds(start, TILE), HD:], grad, (1, 1))
            score_grad = (weights.astype(F32) * ((prob_grad - delta) * scale)).astype(BF16)
            value_acc[pl.ds(start, TILE), :] += dot(weights, grad, (1, 0))
            key_acc[pl.ds(start, TILE), :] += dot(score_grad, query, (1, 0))
            query_grad = query_grad + dot(keys, score_grad, (0, 0))
        query_acc[pl.ds(base, TILE), :] = query_grad.T.astype(BF16)

    @pl.loop(0, tiles)
    def _(tile):
        near = [tile + HALO, tile + HALO - 1, tile + HALO + 1]

        @pl.when(counts_ref[tile] >= NB)
        def _():
            tile_step(tile, near + [slots_ref[tile * NB + NB - 1]])

        @pl.when(counts_ref[tile] < NB)
        def _():
            tile_step(tile, near)

    for at in range(HALO):
        for place, flip, ref in zip(places, flips, query_grad_refs):
            ref[at] = query_acc[tile_rows(place - 1, flip, at), :]
        for place, flip, ref in zip(places, flips, kv_grad_refs):
            rows = tile_rows(place, flip, at)
            ref[at, :, :HD] = key_acc[rows, :].astype(ref.dtype)
            ref[at, :, HD:] = value_acc[rows, :].astype(ref.dtype)


def attention(slots, counts, odd, delta, qg_blocks, kv_blocks):
    n = len(qg_blocks)
    tiles = n * HALO
    rows = tiles * TILE
    window = rows + 2 * HALO * TILE
    vmem = pl.BlockSpec(memory_space=pltpu.VMEM)
    smem = pl.BlockSpec(memory_space=pltpu.SMEM)

    def blocks(count, width, dtype):
        return [jax.ShapeDtypeStruct((HALO, TILE, width), dtype)] * count

    out = pl.pallas_call(
        functools.partial(attention_kernel, n),
        out_shape=blocks(n, HD, BF16) + blocks(n, 2 * HD, F32) + blocks(2, 2 * HD, BF16),
        in_specs=[smem] * 3 + [vmem] * (1 + len(qg_blocks) + len(kv_blocks)),
        out_specs=[vmem] * (2 * n + 2),
        scratch_shapes=[
            pltpu.VMEM((rows, 2 * HD), BF16),
            pltpu.VMEM((window, 2 * HD), BF16),
            pltpu.VMEM((rows, HD), BF16),
            pltpu.VMEM((window, HD), F32),
            pltpu.VMEM((window, HD), F32),
            pltpu.VMEM((NB, TILE, TILE), F32),
        ],
        compiler_params=pltpu.CompilerParams(vmem_limit_bytes=40 * 2**20),
        cost_estimate=pl.CostEstimate(
            flops=2 * 5 * rows * NB * TILE * HD * 2,
            bytes_accessed=rows * HD * 30,
            transcendentals=rows * NB * TILE,
        ),
    )(slots.reshape(-1), counts, odd, delta.reshape(tiles, 1, TILE), *qg_blocks, *kv_blocks)
    return out[:n], out[n : 2 * n], out[2 * n :]


def shifted(block, axis, distance):
    count = lax.axis_size(axis)
    return lax.ppermute(block, axis, [(i, (i + distance) % count) for i in range(count)])


def swapped(block, axis, bit):
    count = lax.axis_size(axis)
    return lax.ppermute(block, axis, [(i, i ^ bit) for i in range(count)])


def head_cols(array, head):
    return lax.dynamic_slice_in_dim(array, head * HD, HD, 1)


def tables(neighbours, counts, first, tiles, tiles_all):
    ids = first + jnp.arange(tiles)
    slots = (neighbours[ids] - (first - HALO)) % tiles_all
    return slots.astype(jnp.int32), counts[ids].astype(jnp.int32)


def chip_sum(stack, projection, target):
    core = lax.axis_index("head") % 2
    width = projection.shape[2] // 4
    weights = lax.dynamic_slice_in_dim(projection, target * 2 * width, 2 * width, 2)
    term = jnp.einsum("cik,ckm->im", stack, weights, preferred_element_type=F32).astype(BF16)
    sent = lax.dynamic_slice_in_dim(term, (1 - core) * width, width, 1)
    kept = lax.dynamic_slice_in_dim(term, core * width, width, 1)
    return kept.astype(F32) + swapped(sent, "head", 1).astype(F32)


def scattered_over_heads(stack, projection):
    term = jnp.einsum("cik,ckm->im", stack, projection, preferred_element_type=F32)
    return lax.psum_scatter(term.astype(BF16), "head", scatter_dimension=1, tiled=True)


def after(arrays, awaited):
    return lax.optimization_barrier((tuple(arrays), tuple(awaited)))[0]


def local(
    query_rows, key_rows, value_rows, output_rows, output_grad, projection, neighbours, counts
):
    seq_count = lax.axis_size("seq")
    place = lax.axis_index("seq")
    rows_dev = query_rows.shape[0]
    tiles_dev = rows_dev // TILE
    tiles_all = tiles_dev * seq_count
    heads_dev = query_rows.shape[1] // HD
    deltas = jnp.sum(
        (output_grad.astype(F32) * output_rows.astype(F32)).reshape(rows_dev, heads_dev, HD), axis=-1
    ).T
    if heads_dev % 2 or seq_count % 2 or tiles_dev != HALO:
        grads = ([], [], [])
        slots, live = tables(neighbours, counts, place * tiles_dev, tiles_dev, tiles_all)
        for head in range(heads_dev):
            qg = jnp.concatenate([head_cols(query_rows, head), head_cols(output_grad, head)], 1)
            kv = jnp.concatenate([head_cols(key_rows, head), head_cols(value_rows, head)], 1)
            window = [kv, shifted(kv, "seq", 1), shifted(kv, "seq", -1)]
            (query_grad,), (own,), (to_prev, to_next) = attention(
                slots, live, jnp.zeros((1,), jnp.int32), deltas[head], [qg], window
            )
            own = own + shifted(to_prev, "seq", -1).astype(F32) + shifted(to_next, "seq", 1).astype(F32)
            own = own.astype(BF16).reshape(rows_dev, 2 * HD)
            query_grad = query_grad.reshape(rows_dev, HD)
            for into, block in zip(grads, (query_grad, own[:, :HD], own[:, HD:])):
                into.append(block)
        stack = jnp.stack([jnp.concatenate(blocks, 1) for blocks in grads])
        return scattered_over_heads(stack, projection)

    odd = place % 2
    even = odd == 0
    half = heads_dev // 2
    first = (place - odd) * tiles_dev
    slots, live = tables(neighbours, counts, first, 2 * tiles_dev, tiles_all)

    def in_order(mine, other):
        return jnp.where(even, mine, other), jnp.where(even, other, mine)

    def both(left, right, head):
        return jnp.concatenate([head_cols(left, head), head_cols(right, head)], 1)

    kept, sent = odd * half, (1 - odd) * half
    kv_kept = [both(key_rows, value_rows, kept + step) for step in range(half)]
    kv_sent = [both(key_rows, value_rows, sent + step) for step in range(half)]
    qg_kept = [both(query_rows, output_grad, kept + step) for step in range(half)]
    qg_sent = [both(query_rows, output_grad, sent + step) for step in range(half)]

    def outward(block, sign):
        route = [(i, (i + 2 * sign * (2 * (i % 2) - 1)) % seq_count) for i in range(seq_count)]
        return lax.ppermute(block, "seq", route)

    kv_got = [swapped(kv_sent[0], "seq", 1)]
    halos = [(outward(kv_kept[0], 1), outward(kv_got[0], -1))]
    delta_sent = lax.dynamic_slice_in_dim(deltas, sent, half, 0)
    qg_got = []
    for step in range(half):
        wave = [qg_sent[step]] + kv_sent[step + 1 : step + 2]
        if step == 0:
            wave.append(delta_sent)
        wave = [swapped(block, "seq", 1) for block in after(wave, [kv_got[step]])]
        qg_got.append(wave[0])
        if step == 0:
            delta_got = wave[-1]
        if step + 1 < half:
            kv_got.append(wave[1])
            (own_block,) = after([kv_kept[step + 1]], [halos[step][0]])
            (got_block,) = after([kv_got[step + 1]], [halos[step][1]])
            halos.append((outward(own_block, 1), outward(got_block, -1)))
    delta_kept = lax.dynamic_slice_in_dim(deltas, kept, half, 0)
    delta_pair = jnp.concatenate(in_order(delta_kept, delta_got), 1)
    odd_ref = odd.astype(jnp.int32).reshape(1)

    query_mine, query_sent, kv_mine, kv_other = [], [], [], []
    for step in range(half):
        window = [kv_kept[step], kv_got[step], *halos[step]]
        query_grad, (own, other), (back_own, back_other) = attention(
            slots, live, odd_ref, delta_pair[step], [qg_kept[step], qg_got[step]], window
        )
        query_mine.append(query_grad[0])
        query_sent.append(query_grad[1])
        if step + 1 < half:
            back_other, back_own = outward(back_other, 1), outward(back_own, -1)
            kv_mine.append((own + back_own.astype(F32)).astype(BF16))
            kv_other.append(swapped((other + back_other.astype(F32)).astype(BF16), "seq", 1))
        else:
            mine, others = [], []
            near = None
            for at in range(HALO):
                pair = back_other[at], back_own[at]
                if near is not None:
                    pair = [after([block], [before])[0] for block, before in zip(pair, near)]
                near = outward(pair[0], 1), outward(pair[1], -1)
                others.append(swapped((other[at] + near[0].astype(F32)).astype(BF16), "seq", 1))
                mine.append((own[at] + near[1].astype(F32)).astype(BF16))
            kv_mine.append(mine)
            kv_other.append(others)
    query_got = swapped(jnp.concatenate(query_sent, 2), "seq", 1)

    chip = lax.axis_index("head") // 2
    results = []
    sent_sum = None
    for at in range(HALO):
        parts = [in_order(jnp.concatenate([block[at] for block in query_mine], 1), query_got[at])]
        for cols in (slice(0, HD), slice(HD, 2 * HD)):
            parts.append(
                in_order(
                    jnp.concatenate([blocks[at][:, cols] for blocks in kv_mine], 1),
                    jnp.concatenate([blocks[at][:, cols] for blocks in kv_other], 1),
                )
            )
        if lax.axis_size("head") != 4:
            stack = jnp.stack([jnp.concatenate(part, 1) for part in parts])
            results.append(scattered_over_heads(stack, projection))
            continue
        if sent_sum is not None:
            parts = [after(part, [sent_sum]) for part in parts]
        stack = jnp.stack([jnp.concatenate(part, 1) for part in parts])
        sent_sum = chip_sum(stack, projection, 1 - chip).astype(BF16)
        far = swapped(sent_sum, "head", 2)
        results.append((stack, far))
    if lax.axis_size("head") == 4:
        results = [
            (chip_sum(stack, projection, chip) + far.astype(F32)).astype(BF16)
            for stack, far in results
        ]
    return jnp.concatenate(in_order(results[0], results[1]), 0)


def solution(mesh):
    in_specs = (
        P("seq", "head"),
        P("seq", "head"),
        P("seq", "head"),
        P("seq", "head"),
        P("seq", "head"),
        P(None, "head", None),
        P(),
        P(),
    )
    out_specs = P("seq", "head")
    return jax.shard_map(local, mesh=mesh, in_specs=in_specs, out_specs=out_specs, check_vma=False)
```

```python
import functools
import math

import jax
import jax.numpy as jnp
from jax import lax
from jax.experimental import pallas as pl
from jax.experimental.pallas import tpu as pltpu
from jax.sharding import PartitionSpec as P

HD = 128
TILE = 384
NB = 4
HALO = 2
F32 = jnp.float32
BF16 = jnp.bfloat16


def dot(a, b, dims):
    return lax.dot_general(a, b, ((dims[:1], dims[1:]), ((), ())), preferred_element_type=F32)


def attention_kernel(own_blocks, slots_ref, counts_ref, odd_ref, delta_ref, *refs):
    n = own_blocks
    tiles = n * HALO
    qg_refs, kv_refs, refs = refs[:n], refs[n : 2 * n + 2], refs[2 * n + 2 :]
    query_grad_refs, kv_grad_refs, refs = refs[:n], refs[n : 2 * n + 2], refs[2 * n + 2 :]
    qg, kv, query_acc, key_acc, value_acc, work = refs
    rows_block = HALO * TILE
    if n == 2:
        odd = odd_ref[0]
        places = [1 + odd, 2 - odd, 3 * (1 - odd), 3 * odd]
        flips = [odd, 1 - odd, odd, 1 - odd]
    else:
        places, flips = [1, 0, 2], [0, 0, 0]

    def tile_rows(place, flip, at):
        in_block = flip if at == 0 else 1 - flip
        return pl.ds(pl.multiple_of((place * HALO + in_block) * TILE, TILE), TILE)

    for place, ref in zip(places, qg_refs):
        qg[pl.ds(pl.multiple_of((place - 1) * rows_block, TILE), rows_block), :] = ref[...]
    for place, ref in zip(places, kv_refs):
        kv[pl.ds(pl.multiple_of(place * rows_block, TILE), rows_block), :] = ref[...]
    key_acc[...] = jnp.zeros_like(key_acc)
    value_acc[...] = jnp.zeros_like(value_acc)
    scale = HD ** (-0.5)
    exponent = scale * math.log2(math.e)

    def tile_step(tile, slot_places):
        base = pl.multiple_of(tile * TILE, TILE)
        query = qg[pl.ds(base, TILE), :HD]
        grad = qg[pl.ds(base, TILE), HD:]
        delta = delta_ref[tile]
        starts = [pl.multiple_of(place * TILE, TILE) for place in slot_places]
        peak = None
        for j, start in enumerate(starts):
            scores = dot(kv[pl.ds(start, TILE), :HD], query, (1, 1))
            work[j] = scores
            top = jnp.max(scores, axis=0, keepdims=True)
            peak = top if peak is None else jnp.maximum(peak, top)
        total = jnp.zeros_like(peak)
        for j in range(len(starts)):
            raised = jnp.exp2((work[j] - peak) * exponent)
            work[j] = raised
            total = total + jnp.sum(raised, axis=0, keepdims=True)
        inverse = 1.0 / total
        query_grad = jnp.zeros((HD, TILE), F32)
        for j, start in enumerate(starts):
            keys = kv[pl.ds(start, TILE), :HD]
            weights = (work[j] * inverse).astype(BF16)
            prob_grad = dot(kv[pl.ds(start, TILE), HD:], grad, (1, 1))
            score_grad = (weights.astype(F32) * ((prob_grad - delta) * scale)).astype(BF16)
            value_acc[pl.ds(start, TILE), :] += dot(weights, grad, (1, 0))
            key_acc[pl.ds(start, TILE), :] += dot(score_grad, query, (1, 0))
            query_grad = query_grad + dot(keys, score_grad, (0, 0))
        query_acc[pl.ds(base, TILE), :] = query_grad.T.astype(BF16)

    @pl.loop(0, tiles)
    def _(tile):
        near = [tile + HALO, tile + HALO - 1, tile + HALO + 1]

        @pl.when(counts_ref[tile] >= NB)
        def _():
            tile_step(tile, near + [slots_ref[tile * NB + NB - 1]])

        @pl.when(counts_ref[tile] < NB)
        def _():
            tile_step(tile, near)

    for at in range(HALO):
        for place, flip, ref in zip(places, flips, query_grad_refs):
            ref[at] = query_acc[tile_rows(place - 1, flip, at), :]
        for place, flip, ref in zip(places, flips, kv_grad_refs):
            rows = tile_rows(place, flip, at)
            ref[at, :, :HD] = key_acc[rows, :].astype(ref.dtype)
            ref[at, :, HD:] = value_acc[rows, :].astype(ref.dtype)


def attention(slots, counts, odd, delta, qg_blocks, kv_blocks):
    n = len(qg_blocks)
    tiles = n * HALO
    rows = tiles * TILE
    window = rows + 2 * HALO * TILE
    vmem = pl.BlockSpec(memory_space=pltpu.VMEM)
    smem = pl.BlockSpec(memory_space=pltpu.SMEM)

    def blocks(count, width, dtype):
        return [jax.ShapeDtypeStruct((HALO, TILE, width), dtype)] * count

    out = pl.pallas_call(
        functools.partial(attention_kernel, n),
        out_shape=blocks(n, HD, BF16) + blocks(n, 2 * HD, F32) + blocks(2, 2 * HD, BF16),
        in_specs=[smem] * 3 + [vmem] * (1 + len(qg_blocks) + len(kv_blocks)),
        out_specs=[vmem] * (2 * n + 2),
        scratch_shapes=[
            pltpu.VMEM((rows, 2 * HD), BF16),
            pltpu.VMEM((window, 2 * HD), BF16),
            pltpu.VMEM((rows, HD), BF16),
            pltpu.VMEM((window, HD), F32),
            pltpu.VMEM((window, HD), F32),
            pltpu.VMEM((NB, TILE, TILE), F32),
        ],
        compiler_params=pltpu.CompilerParams(vmem_limit_bytes=40 * 2**20),
        cost_estimate=pl.CostEstimate(
            flops=2 * 5 * rows * NB * TILE * HD * 2,
            bytes_accessed=rows * HD * 30,
            transcendentals=rows * NB * TILE,
        ),
    )(slots.reshape(-1), counts, odd, delta.reshape(tiles, 1, TILE), *qg_blocks, *kv_blocks)
    return out[:n], out[n : 2 * n], out[2 * n :]


def shifted(block, axis, distance):
    count = lax.axis_size(axis)
    return lax.ppermute(block, axis, [(i, (i + distance) % count) for i in range(count)])


def swapped(block, axis, bit):
    count = lax.axis_size(axis)
    return lax.ppermute(block, axis, [(i, i ^ bit) for i in range(count)])


def head_cols(array, head):
    return lax.dynamic_slice_in_dim(array, head * HD, HD, 1)


def tables(neighbours, counts, first, tiles, tiles_all):
    ids = first + jnp.arange(tiles)
    slots = (neighbours[ids] - (first - HALO)) % tiles_all
    return slots.astype(jnp.int32), counts[ids].astype(jnp.int32)


def chip_term(stack, projection, target):
    width = projection.shape[2] // 4
    weights = lax.dynamic_slice_in_dim(projection, target * 2 * width, 2 * width, 2)
    return jnp.einsum("cik,ckm->im", stack, weights, preferred_element_type=F32).astype(BF16)


def chip_sum(term):
    core = lax.axis_index("head") % 2
    width = term.shape[1] // 2
    sent = lax.dynamic_slice_in_dim(term, (1 - core) * width, width, 1)
    kept = lax.dynamic_slice_in_dim(term, core * width, width, 1)
    return kept.astype(F32) + swapped(sent, "head", 1).astype(F32)


def scattered_over_heads(stack, projection):
    term = jnp.einsum("cik,ckm->im", stack, projection, preferred_element_type=F32)
    return lax.psum_scatter(term.astype(BF16), "head", scatter_dimension=1, tiled=True)


def after(arrays, awaited):
    return lax.optimization_barrier((tuple(arrays), tuple(awaited)))[0]


def local(
    query_rows, key_rows, value_rows, output_rows, output_grad, projection, neighbours, counts
):
    seq_count = lax.axis_size("seq")
    place = lax.axis_index("seq")
    rows_dev = query_rows.shape[0]
    tiles_dev = rows_dev // TILE
    tiles_all = tiles_dev * seq_count
    heads_dev = query_rows.shape[1] // HD

    def head_delta(head):
        grad, output = head_cols(output_grad, head), head_cols(output_rows, head)
        return jnp.sum(grad.astype(F32) * output.astype(F32), axis=1)

    if heads_dev % 2 or seq_count % 2 or tiles_dev != HALO:
        grads = ([], [], [])
        slots, live = tables(neighbours, counts, place * tiles_dev, tiles_dev, tiles_all)
        for head in range(heads_dev):
            qg = jnp.concatenate([head_cols(query_rows, head), head_cols(output_grad, head)], 1)
            kv = jnp.concatenate([head_cols(key_rows, head), head_cols(value_rows, head)], 1)
            window = [kv, shifted(kv, "seq", 1), shifted(kv, "seq", -1)]
            (query_grad,), (own,), (to_prev, to_next) = attention(
                slots, live, jnp.zeros((1,), jnp.int32), head_delta(head), [qg], window
            )
            own = own + shifted(to_prev, "seq", -1).astype(F32) + shifted(to_next, "seq", 1).astype(F32)
            own = own.astype(BF16).reshape(rows_dev, 2 * HD)
            query_grad = query_grad.reshape(rows_dev, HD)
            for into, block in zip(grads, (query_grad, own[:, :HD], own[:, HD:])):
                into.append(block)
        stack = jnp.stack([jnp.concatenate(blocks, 1) for blocks in grads])
        return scattered_over_heads(stack, projection)

    odd = place % 2
    even = odd == 0
    half = heads_dev // 2
    first = (place - odd) * tiles_dev
    slots, live = tables(neighbours, counts, first, 2 * tiles_dev, tiles_all)

    def in_order(mine, other):
        return jnp.where(even, mine, other), jnp.where(even, other, mine)

    def both(left, right, head):
        return jnp.concatenate([head_cols(left, head), head_cols(right, head)], 1)

    kept, sent = odd * half, (1 - odd) * half

    def outward(block, sign):
        route = [(i, (i + 2 * sign * (2 * (i % 2) - 1)) % seq_count) for i in range(seq_count)]
        return lax.ppermute(block, "seq", route)

    kv_got = [swapped(both(key_rows, value_rows, sent), "seq", 1)]
    kv_kept = [both(key_rows, value_rows, kept)]
    halos = [(outward(kv_kept[0], 1), outward(kv_got[0], -1))]
    kept, sent = after([kept, sent], kv_got)
    qg_kept, qg_got = [], []
    arrived = kv_got[0]
    for step in range(half):
        (block,) = after([both(query_rows, output_grad, sent + step)], [arrived])
        arrived = swapped(block, "seq", 1)
        qg_got.append(arrived)
        qg_kept.append(both(query_rows, output_grad, kept + step))
        if step == 0:
            delta_sent = jnp.stack([head_delta(sent + at) for at in range(half)])
            delta_got = swapped(delta_sent, "seq", 1)
        if step + 1 < half:
            (block,) = after([both(key_rows, value_rows, sent + step + 1)], [arrived])
            arrived = swapped(block, "seq", 1)
            kv_got.append(arrived)
            kv_kept.append(both(key_rows, value_rows, kept + step + 1))
            (own_block,) = after([kv_kept[step + 1]], [halos[step][0]])
            (got_block,) = after([kv_got[step + 1]], [halos[step][1]])
            halos.append((outward(own_block, 1), outward(got_block, -1)))
    delta_kept = jnp.stack([head_delta(kept + at) for at in range(half)])
    delta_pair = jnp.concatenate(in_order(delta_kept, delta_got), 1)
    odd_ref = odd.astype(jnp.int32).reshape(1)

    query_mine, query_sent, kv_mine, kv_other = [], [], [], []
    for step in range(half):
        window = [kv_kept[step], kv_got[step], *halos[step]]
        query_grad, (own, other), (back_own, back_other) = attention(
            slots, live, odd_ref, delta_pair[step], [qg_kept[step], qg_got[step]], window
        )
        query_mine.append(query_grad[0])
        query_sent.append(query_grad[1])
        if step + 1 < half:
            back_other, back_own = outward(back_other, 1), outward(back_own, -1)
            kv_mine.append((own + back_own.astype(F32)).astype(BF16))
            kv_other.append(swapped((other + back_other.astype(F32)).astype(BF16), "seq", 1))
        else:
            mine, others = [], []
            near = None
            for at in range(HALO):
                pair = back_other[at], back_own[at]
                if near is not None:
                    pair = [after([block], [before])[0] for block, before in zip(pair, near)]
                near = outward(pair[0], 1), outward(pair[1], -1)
                others.append((other[at] + near[0].astype(F32)).astype(BF16))
                mine.append((own[at] + near[1].astype(F32)).astype(BF16))
            kv_mine.append(mine)
            kv_other.append(others)
    query_got = swapped(jnp.concatenate(query_sent, 2), "seq", 1)

    chip = lax.axis_index("head") // 2
    results = []
    term = None
    for at in range(HALO):
        others = [blocks[at] for blocks in kv_other]
        block = others[-1] if term is None else after([others[-1]], [term])[0]
        others[-1] = swapped(block, "seq", 1)
        parts = [in_order(jnp.concatenate([block[at] for block in query_mine], 1), query_got[at])]
        for cols in (slice(0, HD), slice(HD, 2 * HD)):
            parts.append(
                in_order(
                    jnp.concatenate([blocks[at][:, cols] for blocks in kv_mine], 1),
                    jnp.concatenate([block[:, cols] for block in others], 1),
                )
            )
        stack = jnp.stack([jnp.concatenate(part, 1) for part in parts])
        if lax.axis_size("head") == 4:
            term = chip_term(stack, projection, 1 - chip)
            results.append((stack, swapped(chip_sum(term).astype(BF16), "head", 2)))
        else:
            results.append(scattered_over_heads(stack, projection))
    if lax.axis_size("head") == 4:
        results = [
            (chip_sum(chip_term(stack, projection, chip)) + far.astype(F32)).astype(BF16)
            for stack, far in results
        ]
    return jnp.concatenate(in_order(results[0], results[1]), 0)


def solution(mesh):
    in_specs = (
        P("seq", "head"),
        P("seq", "head"),
        P("seq", "head"),
        P("seq", "head"),
        P("seq", "head"),
        P(None, "head", None),
        P(),
        P(),
    )
    out_specs = P("seq", "head")
    return jax.shard_map(local, mesh=mesh, in_specs=in_specs, out_specs=out_specs, check_vma=False)
```

```python
import functools
import math

import jax
import jax.numpy as jnp
from jax import lax
from jax.experimental import pallas as pl
from jax.experimental.pallas import tpu as pltpu
from jax.sharding import PartitionSpec as P

HD = 128
TILE = 384
NB = 4
HALO = 2
F32 = jnp.float32
BF16 = jnp.bfloat16


def dot(a, b, dims):
    return lax.dot_general(a, b, ((dims[:1], dims[1:]), ((), ())), preferred_element_type=F32)


def attention_kernel(own_blocks, slots_ref, counts_ref, odd_ref, delta_ref, *refs):
    n = own_blocks
    tiles = n * HALO
    qg_refs, kv_refs, refs = refs[:n], refs[n : 2 * n + 2], refs[2 * n + 2 :]
    query_grad_refs, kv_grad_refs, refs = refs[:n], refs[n : 2 * n + 2], refs[2 * n + 2 :]
    qg, kv, query_acc, key_acc, value_acc, work = refs
    rows_block = HALO * TILE
    if n == 2:
        odd = odd_ref[0]
        places = [1 + odd, 2 - odd, 3 * (1 - odd), 3 * odd]
        flips = [odd, 1 - odd, odd, 1 - odd]
    else:
        places, flips = [1, 0, 2], [0, 0, 0]

    def tile_rows(place, flip, at):
        in_block = flip if at == 0 else 1 - flip
        return pl.ds(pl.multiple_of((place * HALO + in_block) * TILE, TILE), TILE)

    for place, ref in zip(places, qg_refs):
        qg[pl.ds(pl.multiple_of((place - 1) * rows_block, TILE), rows_block), :] = ref[...]
    for place, ref in zip(places, kv_refs):
        kv[pl.ds(pl.multiple_of(place * rows_block, TILE), rows_block), :] = ref[...]
    key_acc[...] = jnp.zeros_like(key_acc)
    value_acc[...] = jnp.zeros_like(value_acc)
    scale = HD ** (-0.5)
    exponent = scale * math.log2(math.e)

    def tile_step(tile, slot_places):
        base = pl.multiple_of(tile * TILE, TILE)
        query = qg[pl.ds(base, TILE), :HD]
        grad = qg[pl.ds(base, TILE), HD:]
        delta = delta_ref[tile]
        starts = [pl.multiple_of(place * TILE, TILE) for place in slot_places]
        peak = None
        for j, start in enumerate(starts):
            scores = dot(kv[pl.ds(start, TILE), :HD], query, (1, 1))
            work[j] = scores
            top = jnp.max(scores, axis=0, keepdims=True)
            peak = top if peak is None else jnp.maximum(peak, top)
        total = jnp.zeros_like(peak)
        for j in range(len(starts)):
            raised = jnp.exp2((work[j] - peak) * exponent)
            work[j] = raised
            total = total + jnp.sum(raised, axis=0, keepdims=True)
        inverse = 1.0 / total
        query_grad = jnp.zeros((HD, TILE), F32)
        for j, start in enumerate(starts):
            keys = kv[pl.ds(start, TILE), :HD]
            weights = (work[j] * inverse).astype(BF16)
            prob_grad = dot(kv[pl.ds(start, TILE), HD:], grad, (1, 1))
            score_grad = (weights.astype(F32) * ((prob_grad - delta) * scale)).astype(BF16)
            value_acc[pl.ds(start, TILE), :] += dot(weights, grad, (1, 0))
            key_acc[pl.ds(start, TILE), :] += dot(score_grad, query, (1, 0))
            query_grad = query_grad + dot(keys, score_grad, (0, 0))
        query_acc[pl.ds(base, TILE), :] = query_grad.T.astype(BF16)

    @pl.loop(0, tiles)
    def _(tile):
        near = [tile + HALO, tile + HALO - 1, tile + HALO + 1]

        @pl.when(counts_ref[tile] >= NB)
        def _():
            tile_step(tile, near + [slots_ref[tile * NB + NB - 1]])

        @pl.when(counts_ref[tile] < NB)
        def _():
            tile_step(tile, near)

    for at in range(HALO):
        for place, flip, ref in zip(places, flips, query_grad_refs):
            ref[at] = query_acc[tile_rows(place - 1, flip, at), :]
        for place, flip, ref in zip(places, flips, kv_grad_refs):
            rows = tile_rows(place, flip, at)
            ref[at, :, :HD] = key_acc[rows, :].astype(ref.dtype)
            ref[at, :, HD:] = value_acc[rows, :].astype(ref.dtype)


def attention(slots, counts, odd, delta, qg_blocks, kv_blocks):
    n = len(qg_blocks)
    tiles = n * HALO
    rows = tiles * TILE
    window = rows + 2 * HALO * TILE
    vmem = pl.BlockSpec(memory_space=pltpu.VMEM)
    smem = pl.BlockSpec(memory_space=pltpu.SMEM)

    def blocks(count, width, dtype):
        return [jax.ShapeDtypeStruct((HALO, TILE, width), dtype)] * count

    out = pl.pallas_call(
        functools.partial(attention_kernel, n),
        out_shape=blocks(n, HD, BF16) + blocks(n, 2 * HD, F32) + blocks(2, 2 * HD, BF16),
        in_specs=[smem] * 3 + [vmem] * (1 + len(qg_blocks) + len(kv_blocks)),
        out_specs=[vmem] * (2 * n + 2),
        scratch_shapes=[
            pltpu.VMEM((rows, 2 * HD), BF16),
            pltpu.VMEM((window, 2 * HD), BF16),
            pltpu.VMEM((rows, HD), BF16),
            pltpu.VMEM((window, HD), F32),
            pltpu.VMEM((window, HD), F32),
            pltpu.VMEM((NB, TILE, TILE), F32),
        ],
        compiler_params=pltpu.CompilerParams(vmem_limit_bytes=40 * 2**20),
        cost_estimate=pl.CostEstimate(
            flops=2 * 5 * rows * NB * TILE * HD * 2,
            bytes_accessed=rows * HD * 30,
            transcendentals=rows * NB * TILE,
        ),
    )(slots.reshape(-1), counts, odd, delta.reshape(tiles, 1, TILE), *qg_blocks, *kv_blocks)
    return out[:n], out[n : 2 * n], out[2 * n :]


def shifted(block, axis, distance):
    count = lax.axis_size(axis)
    return lax.ppermute(block, axis, [(i, (i + distance) % count) for i in range(count)])


def swapped(block, axis, bit):
    count = lax.axis_size(axis)
    return lax.ppermute(block, axis, [(i, i ^ bit) for i in range(count)])


def head_cols(array, head):
    return lax.dynamic_slice_in_dim(array, head * HD, HD, 1)


def tables(neighbours, counts, first, tiles, tiles_all):
    ids = first + jnp.arange(tiles)
    slots = (neighbours[ids] - (first - HALO)) % tiles_all
    return slots.astype(jnp.int32), counts[ids].astype(jnp.int32)


def chip_term(stack, projection, target):
    width = projection.shape[2] // 4
    weights = lax.dynamic_slice_in_dim(projection, target * 2 * width, 2 * width, 2)
    return jnp.einsum("cik,ckm->im", stack, weights, preferred_element_type=F32).astype(BF16)


def chip_sum(term):
    core = lax.axis_index("head") % 2
    width = term.shape[1] // 2
    sent = lax.dynamic_slice_in_dim(term, (1 - core) * width, width, 1)
    kept = lax.dynamic_slice_in_dim(term, core * width, width, 1)
    return kept.astype(F32) + swapped(sent, "head", 1).astype(F32)


def scattered_over_heads(stack, projection):
    term = jnp.einsum("cik,ckm->im", stack, projection, preferred_element_type=F32)
    return lax.psum_scatter(term.astype(BF16), "head", scatter_dimension=1, tiled=True)


def after(arrays, awaited):
    return lax.optimization_barrier((tuple(arrays), tuple(awaited)))[0]


def local(
    query_rows, key_rows, value_rows, output_rows, output_grad, projection, neighbours, counts
):
    seq_count = lax.axis_size("seq")
    place = lax.axis_index("seq")
    rows_dev = query_rows.shape[0]
    tiles_dev = rows_dev // TILE
    tiles_all = tiles_dev * seq_count
    heads_dev = query_rows.shape[1] // HD
    deltas = jnp.sum(
        (output_grad.astype(F32) * output_rows.astype(F32)).reshape(rows_dev, heads_dev, HD), axis=-1
    ).T
    if heads_dev % 2 or seq_count % 2 or tiles_dev != HALO:
        grads = ([], [], [])
        slots, live = tables(neighbours, counts, place * tiles_dev, tiles_dev, tiles_all)
        for head in range(heads_dev):
            qg = jnp.concatenate([head_cols(query_rows, head), head_cols(output_grad, head)], 1)
            kv = jnp.concatenate([head_cols(key_rows, head), head_cols(value_rows, head)], 1)
            window = [kv, shifted(kv, "seq", 1), shifted(kv, "seq", -1)]
            (query_grad,), (own,), (to_prev, to_next) = attention(
                slots, live, jnp.zeros((1,), jnp.int32), deltas[head], [qg], window
            )
            own = own + shifted(to_prev, "seq", -1).astype(F32) + shifted(to_next, "seq", 1).astype(F32)
            own = own.astype(BF16).reshape(rows_dev, 2 * HD)
            query_grad = query_grad.reshape(rows_dev, HD)
            for into, block in zip(grads, (query_grad, own[:, :HD], own[:, HD:])):
                into.append(block)
        stack = jnp.stack([jnp.concatenate(blocks, 1) for blocks in grads])
        return scattered_over_heads(stack, projection)

    odd = place % 2
    even = odd == 0
    half = heads_dev // 2
    first = (place - odd) * tiles_dev
    slots, live = tables(neighbours, counts, first, 2 * tiles_dev, tiles_all)

    def in_order(mine, other):
        return jnp.where(even, mine, other), jnp.where(even, other, mine)

    def both(left, right, head):
        return jnp.concatenate([head_cols(left, head), head_cols(right, head)], 1)

    kept, sent = odd * half, (1 - odd) * half
    kv_kept = [both(key_rows, value_rows, kept + step) for step in range(half)]
    kv_sent = [both(key_rows, value_rows, sent + step) for step in range(half)]
    qg_kept = [both(query_rows, output_grad, kept + step) for step in range(half)]
    qg_sent = [both(query_rows, output_grad, sent + step) for step in range(half)]

    def outward(block, sign):
        route = [(i, (i + 2 * sign * (2 * (i % 2) - 1)) % seq_count) for i in range(seq_count)]
        return lax.ppermute(block, "seq", route)

    kv_got = [swapped(kv_sent[0], "seq", 1)]
    halos = [(outward(kv_kept[0], 1), outward(kv_got[0], -1))]
    delta_sent = lax.dynamic_slice_in_dim(deltas, sent, half, 0)
    qg_got = []
    for step in range(half):
        wave = [qg_sent[step]] + kv_sent[step + 1 : step + 2]
        if step == 0:
            wave.append(delta_sent)
        wave = [swapped(block, "seq", 1) for block in after(wave, [kv_got[step]])]
        qg_got.append(wave[0])
        if step == 0:
            delta_got = wave[-1]
        if step + 1 < half:
            kv_got.append(wave[1])
            (own_block,) = after([kv_kept[step + 1]], [halos[step][0]])
            (got_block,) = after([kv_got[step + 1]], [halos[step][1]])
            halos.append((outward(own_block, 1), outward(got_block, -1)))
    delta_kept = lax.dynamic_slice_in_dim(deltas, kept, half, 0)
    delta_pair = jnp.concatenate(in_order(delta_kept, delta_got), 1)
    odd_ref = odd.astype(jnp.int32).reshape(1)

    query_mine, query_sent, kv_mine, kv_other = [], [], [], []
    for step in range(half):
        window = [kv_kept[step], kv_got[step], *halos[step]]
        query_grad, (own, other), (back_own, back_other) = attention(
            slots, live, odd_ref, delta_pair[step], [qg_kept[step], qg_got[step]], window
        )
        query_mine.append(query_grad[0])
        query_sent.append(query_grad[1])
        if step + 1 < half:
            back_other, back_own = outward(back_other, 1), outward(back_own, -1)
            kv_mine.append((own + back_own.astype(F32)).astype(BF16))
            kv_other.append(swapped((other + back_other.astype(F32)).astype(BF16), "seq", 1))
        else:
            mine, others = [], []
            near = None
            for at in range(HALO):
                pair = back_other[at], back_own[at]
                if near is not None:
                    pair = [after([block], [before])[0] for block, before in zip(pair, near)]
                near = outward(pair[0], 1), outward(pair[1], -1)
                others.append((other[at] + near[0].astype(F32)).astype(BF16))
                mine.append((own[at] + near[1].astype(F32)).astype(BF16))
            kv_mine.append(mine)
            kv_other.append(others)
    query_got = swapped(jnp.concatenate(query_sent, 2), "seq", 1)

    chip = lax.axis_index("head") // 2
    results = []
    for at in range(HALO):
        others = [blocks[at] for blocks in kv_other]
        others[-1] = swapped(others[-1], "seq", 1)
        parts = [in_order(jnp.concatenate([block[at] for block in query_mine], 1), query_got[at])]
        for cols in (slice(0, HD), slice(HD, 2 * HD)):
            parts.append(
                in_order(
                    jnp.concatenate([blocks[at][:, cols] for blocks in kv_mine], 1),
                    jnp.concatenate([block[:, cols] for block in others], 1),
                )
            )
        stack = jnp.stack([jnp.concatenate(part, 1) for part in parts])
        if lax.axis_size("head") == 4:
            term = chip_sum(chip_term(stack, projection, 1 - chip)).astype(BF16)
            if results:
                (term,) = after([term], [results[-1][1]])
            results.append((stack, swapped(term, "head", 2)))
        else:
            results.append(scattered_over_heads(stack, projection))
    if lax.axis_size("head") == 4:
        results = [
            (chip_sum(chip_term(stack, projection, chip)) + far.astype(F32)).astype(BF16)
            for stack, far in results
        ]
    return jnp.concatenate(in_order(results[0], results[1]), 0)


def solution(mesh):
    in_specs = (
        P("seq", "head"),
        P("seq", "head"),
        P("seq", "head"),
        P("seq", "head"),
        P("seq", "head"),
        P(None, "head", None),
        P(),
        P(),
    )
    out_specs = P("seq", "head")
    return jax.shard_map(local, mesh=mesh, in_specs=in_specs, out_specs=out_specs, check_vma=False)
```
